32 devices in a mesh: dp: 8 (over z, x), fsdp: 4 (over y, core).
Axes of the slice: x: 2, y: 2, z: 4, core: 2. Of those that a mesh axis runs over, the one named last changes fastest.
Arguments:
- tokens: bfloat16 [640, 197, 384], P(('dp', 'fsdp')), may hold values from -6 to 6
- image_count: int32 [32], P(('dp', 'fsdp')), may hold values from 1 to 20, as said below
- w_qkv: bfloat16 [442368], P(('dp', 'fsdp')), may hold values from -0.3125 to 0.3125
- w_out: bfloat16 [147456], P(('dp', 'fsdp')), may hold values from -1.25 to 1.25
- w_fc1: bfloat16 [589824], P(('dp', 'fsdp')), may hold values from -0.3125 to 0.3125
- w_fc2: bfloat16 [589824], P(('dp', 'fsdp')), may hold values from -0.15625 to 0.15625
- norm_bias: bfloat16 [4608], P(('dp', 'fsdp')), may hold values from -1.5 to 1.5, as said below
- cotangent: bfloat16 [640, 197, 384], P(('dp', 'fsdp')), may hold values from -6 to 6
Outputs:
- output: bfloat16 [640, 197, 384], P(('dp', 'fsdp'))
- grad_tokens: bfloat16 [640, 197, 384], P(('dp', 'fsdp'))
- grad_qkv: float32 [442368], P(('dp', 'fsdp'))
- grad_out: float32 [147456], P(('dp', 'fsdp'))
- grad_fc1: float32 [589824], P(('dp', 'fsdp'))
- grad_fc2: float32 [589824], P(('dp', 'fsdp'))
- grad_norm_bias: float32 [4608], P(('dp', 'fsdp'))
The draws below stay inside these ranges and needn't reach their ends.
Inputs may be any that keep to these rules, and one draw needn't show every extreme that they name: `image_count`: live images among a device's 20 slots, the first ones; some device holds 20. `norm_bias`: gains near one, biases and shifts of either sign.
All inputs are finite; a program needn't handle non-finite values.
Results may differ from the reference program's by a relative error of at most 0.011.
Values may be sent and summed in bfloat16 or wider, within the bound.
A program may use at most 256 MiB of HBM per device.

```python
import math
import jax
import jax.numpy as jnp
from jax import lax

D = 384
HEADS = 6
HEAD_DIM = 64
FF = 1536
SEQ = 197
IMG_DEV = 20
IMGS = 640
N_DP = 8
N_FSDP = 4


def draw_image_count(key, part):
    first, second = jax.random.split(jax.random.fold_in(key, 11))
    shards = N_DP * N_FSDP
    counted = jax.random.randint(first, (shards,), 1, IMG_DEV + 1)
    where = jax.random.randint(second, (), 0, shards)
    return counted.at[where].set(IMG_DEV).astype(jnp.int32)


def draw_norm_bias(key, part):
    first, second = jax.random.split(jax.random.fold_in(key, 23))
    length = 8 * D + FF
    position = jnp.arange(length)
    is_gain = (position < D) | (position >= 5 * D) & (position < 6 * D)
    spread = jnp.clip(jax.random.normal(first, (length,), jnp.float32), -3.0, 3.0) * 0.5
    wobble = jax.random.uniform(second, (length,), jnp.float32, -1.0, 1.0) * 0.3
    values = jnp.where(is_gain, 1.0 + wobble, spread)
    return values.astype(jnp.bfloat16)


def levels(key, extent, pieces, low, high):
    level, own = 1.0, jax.random.fold_in(key, 6)
    for dim, shards_of in pieces:
        heights = jnp.exp(jax.random.uniform(jax.random.fold_in(own, dim), (shards_of,), jnp.float32, low / len(pieces), high / len(pieces)))
        level = level * jnp.repeat(heights, extent[dim] // shards_of).reshape([-1 if axis == dim else 1 for axis in range(len(extent))])
    return level


def bell_draw(own_key, shape, scale, limit, cuts=(), kind=jnp.bfloat16):
    drawn = scale * jax.random.normal(own_key, shape, jnp.float32)
    if cuts:
        drawn = drawn * levels(own_key, shape, cuts, -0.22, 0.18)
    return jnp.clip(drawn, -limit, limit).astype(kind)


def setup_inputs(seed: int = 0) -> dict:
    seeds = jax.random.split(jax.random.key(seed), 9)
    return {
        "tokens": bell_draw(seeds[0], (IMGS, SEQ, D), 1.0, 6.0, ((0, 32),)),
        "image_count": draw_image_count(jax.random.fold_in(seeds[8], 71), 0),
        "w_qkv": bell_draw(seeds[2], (3 * D * D,), D ** -0.5, 0.3125, ((0, 32),)),
        "w_out": bell_draw(seeds[3], (D * D,), (D // 16) ** -0.5, 1.25, ((0, 32),)),
        "w_fc1": bell_draw(seeds[4], (D * FF,), D ** -0.5, 0.3125, ((0, 32),)),
        "w_fc2": bell_draw(seeds[5], (FF * D,), FF ** -0.5, 0.15625, ((0, 32),)),
        "norm_bias": draw_norm_bias(jax.random.fold_in(seeds[8], 71), 0),
        "cotangent": bell_draw(seeds[7], (IMGS, SEQ, D), 1.0, 6.0, ((0, 32),)),
    }


@jax.custom_vjp
def low(v):
    return lax.optimization_barrier(v.astype(jnp.bfloat16)).astype(jnp.float32)

@jax.custom_vjp
def low_back(v):
    return v

def low_keep(v):
    return (low(v), None)

def low_pass(kept, grad):
    return (grad,)

def back_keep(v):
    return (v, None)

def back_low(kept, grad):
    return (low(grad),)
low.defvjp(low_keep, low_pass)
low_back.defvjp(back_keep, back_low)
highest = lax.Precision.HIGHEST
epsilon = 1e-06

def layer_norm(values, gain, shift):
    center = values - lax.optimization_barrier(jnp.mean(values, axis=-1, keepdims=True))
    spread = lax.optimization_barrier(jnp.mean(center * center, axis=-1, keepdims=True))
    return center * lax.rsqrt(spread + epsilon) * gain + shift

def block(inputs, alive, wqkv, wout, wup, wdown, small):
    cuts = [D, 2 * D, 3 * D, 4 * D, 5 * D, 6 * D, 7 * D, 7 * D + FF]
    gain_one, shift_one, bias_q, bias_v, bias_o, gain_two, shift_two, bias_up, bias_down = jnp.split(small, cuts)
    images = inputs.shape[0]
    scale = 1.0 / math.sqrt(HEAD_DIM)
    normed = low(layer_norm(inputs, gain_one, shift_one))
    project = jnp.einsum('isd,de->ise', normed, wqkv, precision=highest)
    queries = low(low_back(project[..., :D] + bias_q)).reshape(images, SEQ, HEADS, HEAD_DIM)
    key_part = low(low_back(project[..., D:2 * D])).reshape(images, SEQ, HEADS, HEAD_DIM)
    value_part = low(low_back(project[..., 2 * D:] + bias_v)).reshape(images, SEQ, HEADS, HEAD_DIM)
    scores = low_back(jnp.einsum('ishd,ithd->ihst', queries, key_part, precision=highest) * scale)
    attend = jax.nn.softmax(scores, axis=-1)
    mixed = jnp.einsum('ihst,ithd->ishd', low(attend), value_part, precision=highest).reshape(images, SEQ, D)
    mixed = low(low_back(mixed))
    branch = low_back(jnp.einsum('isd,de->ise', mixed, wout, precision=highest) + bias_o)
    middle = inputs + branch
    second = low(layer_norm(middle, gain_two, shift_two))
    hidden = low_back(jnp.einsum('isd,df->isf', second, wup, precision=highest) + bias_up)
    active = low(jax.nn.gelu(hidden, approximate=False))
    update = low_back(jnp.einsum('isf,fd->isd', active, wdown, precision=highest) + bias_down)
    return (middle + update) * alive[:, None, None]

def reference(tokens, image_count, w_qkv, w_out, w_fc1, w_fc2, norm_bias, cotangent):
    shards = N_DP * N_FSDP
    slot = jnp.arange(IMGS, dtype=jnp.int32)
    owner = (slot // IMG_DEV).astype(jnp.int32)
    alive = (slot % IMG_DEV < image_count[owner]).astype(jnp.float32).reshape(shards, IMG_DEV)
    inputs = tokens.astype(jnp.float32).reshape(shards, IMG_DEV, SEQ, D)
    params = (w_qkv.astype(jnp.float32), w_out.astype(jnp.float32), w_fc1.astype(jnp.float32), w_fc2.astype(jnp.float32), norm_bias.astype(jnp.float32))

    def forward(values, wqkv, wout, wup, wdown, small):
        matrices = (wqkv.reshape(D, 3 * D), wout.reshape(D, D), wup.reshape(D, FF), wdown.reshape(FF, D))
        checked = jax.checkpoint(block)

        def one_group(pair):
            return checked(pair[0], pair[1], matrices[0], matrices[1], matrices[2], matrices[3], small)
        return lax.map(one_group, (values, alive))
    result, pull = jax.vjp(forward, inputs, *params)
    grads = pull(cotangent.astype(jnp.float32).reshape(result.shape))
    output = result.reshape(IMGS, SEQ, D).astype(jnp.bfloat16)
    grad_tokens = grads[0].reshape(IMGS, SEQ, D).astype(jnp.bfloat16)
    return (output, grad_tokens, grads[1], grads[2], grads[3], grads[4], grads[5])
```

```python
import math

import jax
import jax.numpy as jnp
from jax import lax
from jax.experimental import pallas as pl
from jax.experimental.pallas import tpu as pltpu
from jax.sharding import PartitionSpec as P

HEADS = 6
HEAD_DIM = 64
EPS = 1e-06
F32 = jnp.float32
BF16 = jnp.bfloat16


def mm(a, b):
    return lax.dot_general(a, b, (((1,), (0,)), ((), ())), preferred_element_type=F32)


def mm_t(a, b):
    return lax.dot_general(a, b, (((1,), (1,)), ((), ())), preferred_element_type=F32)


def t_mm(a, b):
    return lax.dot_general(a, b, (((0,), (0,)), ((), ())), preferred_element_type=F32)


def norm_parts(values, width):
    mean = jnp.sum(values, axis=-1, keepdims=True) * (1.0 / width)
    center = values - mean
    var = jnp.sum(center * center, axis=-1, keepdims=True) * (1.0 / width)
    inverse = lax.rsqrt(var + EPS)
    return center * inverse, inverse


def norm_back(upstream, normed, inverse, gain, width):
    scaled = upstream * gain
    m1 = jnp.sum(scaled, axis=-1, keepdims=True) * (1.0 / width)
    m2 = jnp.sum(scaled * normed, axis=-1, keepdims=True) * (1.0 / width)
    return inverse * (scaled - m1 - normed * m2)


def gelu_both(z):
    ez = jnp.exp(-0.5 * z * z)
    t = 1.0 / (1.0 + (0.3275911 * 0.7071067811865476) * jnp.abs(z))
    poly = ((((1.061405429 * t - 1.453152027) * t + 1.421413741) * t - 0.284496736) * t + 0.254829592) * t
    half = 0.5 * poly * ez
    cumul = jnp.where(z >= 0.0, 1.0 - half, half)
    return z * cumul, cumul + z * (ez * 0.3989422804014327)


def layer_kernel(
    count_ref, x_ref, ct_ref, wqkv_ref, wout_ref, wup_ref, wdown_ref, small_ref, bup_ref,
    out_ref, gx_ref, gqkv_ref, gout_ref, gup_ref, gdown_ref, gsmall_ref, gbup_ref,
    xs, cs, n1s, qs, ks, vs, pbs, os_, y1s, n2s, a1s, a2s, acts, dzs, dos, dqkvs,
):
    step = pl.program_id(0)
    seq, width = x_ref.shape[1], x_ref.shape[2]
    rows = xs.shape[0]
    hidden = wup_ref.shape[1]
    scale = 1.0 / math.sqrt(HEAD_DIM)

    @pl.when(step == 0)
    def _():
        xs[...] = jnp.zeros_like(xs)
        cs[...] = jnp.zeros_like(cs)
        for ref in (gqkv_ref, gout_ref, gup_ref, gdown_ref, gsmall_ref, gbup_ref):
            ref[...] = jnp.zeros_like(ref)

    live = step < count_ref[0]

    @pl.when(jnp.logical_not(live))
    def _():
        out_ref[...] = jnp.zeros_like(out_ref)
        gx_ref[...] = jnp.zeros_like(gx_ref)

    @pl.when(live)
    def _():
        xs[0:seq, :] = x_ref[0]
        cs[0:seq, :] = ct_ref[0]
        g1, c1 = small_ref[0:1, :], small_ref[1:2, :]
        bq, bv, bo = small_ref[2:3, :], small_ref[3:4, :], small_ref[4:5, :]
        g2, c2, b2 = small_ref[5:6, :], small_ref[6:7, :], small_ref[7:8, :]
        n1, inv1 = norm_parts(xs[...].astype(F32), width)
        n1s[...] = n1
        a1s[...] = (n1 * g1 + c1).astype(BF16)
        qs[...] = (mm(a1s[...], wqkv_ref[:, :width]) + bq).astype(BF16)
        ks[...] = mm(a1s[...], wqkv_ref[:, width : 2 * width]).astype(BF16)
        vs[...] = (mm(a1s[...], wqkv_ref[:, 2 * width :]) + bv).astype(BF16)
        lane = lax.broadcasted_iota(jnp.int32, (rows, 2 * HEAD_DIM), 1)
        halves = (lane < HEAD_DIM, lane >= HEAD_DIM)
        keyrow = lax.broadcasted_iota(jnp.int32, (rows, rows), 0)
        zero = jnp.zeros((rows, 2 * HEAD_DIM), BF16)
        for pair in range(HEADS // 2):
            cols = slice(pair * 2 * HEAD_DIM, (pair + 1) * 2 * HEAD_DIM)
            qp, kp, vp = qs[:, cols], ks[:, cols], vs[:, cols]
            both = None
            for h in range(2):
                km = jnp.where(halves[h], kp, zero)
                vm = jnp.where(halves[h], vp, zero)
                scores = mm_t(km, qp) * scale
                scores = jnp.where(keyrow < seq, scores, -1e30)
                top = jnp.max(scores, axis=0, keepdims=True)
                expo = jnp.exp(scores - top)
                total = jnp.sum(expo, axis=0, keepdims=True)
                prob = expo * (1.0 / total)
                pbs[pair * 2 + h] = prob.astype(BF16)
                part = t_mm(pbs[pair * 2 + h], vm)
                both = part if both is None else both + part
            os_[:, cols] = both.astype(BF16)
        y1 = xs[...].astype(F32) + (mm(os_[...], wout_ref[...]) + bo)
        y1s[...] = y1
        n2, inv2 = norm_parts(y1, width)
        n2s[...] = n2
        a2s[...] = (n2 * g2 + c2).astype(BF16)
        tile = 256
        for j in range(hidden // tile):
            cols = slice(j * tile, (j + 1) * tile)
            z = mm(a2s[...], wup_ref[:, cols]) + bup_ref[:, cols]
            act, slope = gelu_both(z)
            acts[:, cols] = act.astype(BF16)
            dz = (mm_t(cs[...], wdown_ref[cols, :]) * slope).astype(BF16)
            dzs[:, cols] = dz
            gbup_ref[:, cols] += jnp.sum(dz.astype(F32), axis=0, keepdims=True)
        y = y1s[...] + mm(acts[...], wdown_ref[...]) + b2
        out_ref[0] = y[:seq].astype(BF16)
        gdown_ref[...] += t_mm(acts[...], cs[...])
        gup_ref[...] += t_mm(a2s[...], dzs[...])
        da2 = mm_t(dzs[...], wup_ref[...])
        ct = cs[...].astype(F32)
        n2 = n2s[...]
        gsmall_ref[7:8, :] += jnp.sum(ct, axis=0, keepdims=True)
        gsmall_ref[5:6, :] += jnp.sum(da2 * n2, axis=0, keepdims=True)
        gsmall_ref[6:7, :] += jnp.sum(da2, axis=0, keepdims=True)
        dy1 = ct + norm_back(da2, n2, inv2, g2, width)
        y1s[...] = dy1
        da = dy1.astype(BF16)
        gsmall_ref[4:5, :] += jnp.sum(da.astype(F32), axis=0, keepdims=True)
        gout_ref[...] += t_mm(os_[...], da)
        dos[...] = mm_t(da, wout_ref[...]).astype(BF16)
        for pair in range(HEADS // 2):
            cols = slice(pair * 2 * HEAD_DIM, (pair + 1) * 2 * HEAD_DIM)
            qp, kp, vp, dop = qs[:, cols], ks[:, cols], vs[:, cols], dos[:, cols]
            dq = dk = dv = None
            for h in range(2):
                qm = jnp.where(halves[h], qp, zero)
                km = jnp.where(halves[h], kp, zero)
                vm = jnp.where(halves[h], vp, zero)
                dom = jnp.where(halves[h], dop, zero)
                pb = pbs[pair * 2 + h]
                prob = pb.astype(F32)
                dp = mm_t(vm, dop)
                inner = jnp.sum(prob * dp, axis=0, keepdims=True)
                ds = (prob * (dp - inner)).astype(BF16)
                dv_h = mm(pb, dom)
                dk_h = mm(ds, qm)
                dq_h = t_mm(ds, km)
                dq = dq_h if dq is None else dq + dq_h
                dk = dk_h if dk is None else dk + dk_h
                dv = dv_h if dv is None else dv + dv_h
            base = pair * 2 * HEAD_DIM
            dqkvs[:, base : base + 2 * HEAD_DIM] = (dq * scale).astype(BF16)
            dqkvs[:, width + base : width + base + 2 * HEAD_DIM] = (dk * scale).astype(BF16)
            dqkvs[:, 2 * width + base : 2 * width + base + 2 * HEAD_DIM] = dv.astype(BF16)
        gsmall_ref[2:3, :] += jnp.sum(dqkvs[:, :width].astype(F32), axis=0, keepdims=True)
        gsmall_ref[3:4, :] += jnp.sum(dqkvs[:, 2 * width :].astype(F32), axis=0, keepdims=True)
        gqkv_ref[...] += t_mm(a1s[...], dqkvs[...])
        da1 = mm_t(dqkvs[...], wqkv_ref[...])
        n1 = n1s[...]
        gsmall_ref[0:1, :] += jnp.sum(da1 * n1, axis=0, keepdims=True)
        gsmall_ref[1:2, :] += jnp.sum(da1, axis=0, keepdims=True)
        gx = y1s[...] + norm_back(da1, n1, inv1, g1, width)
        gx_ref[0] = gx[:seq].astype(BF16)


def run_layer(count, tokens, cotangent, wqkv, wout, wup, wdown, small, bup):
    slots, seq, width = tokens.shape
    hidden = wup.shape[1]
    rows = (seq + 15) // 16 * 16

    def whole(shape):
        return pl.BlockSpec(shape, lambda i, c: (0,) * len(shape), pipeline_mode=pl.Buffered(1))

    def image():
        return pl.BlockSpec((1, seq, width), lambda i, c: (i, 0, 0))

    return pl.pallas_call(
        layer_kernel,
        grid_spec=pltpu.PrefetchScalarGridSpec(
            num_scalar_prefetch=1,
            grid=(slots,),
            in_specs=[
                image(), image(),
                whole((width, 3 * width)), whole((width, width)), whole((width, hidden)),
                whole((hidden, width)), whole((8, width)), whole((1, hidden)),
            ],
            out_specs=[
                image(), image(),
                whole((width, 3 * width)), whole((width, width)), whole((width, hidden)),
                whole((hidden, width)), whole((8, width)), whole((1, hidden)),
            ],
            scratch_shapes=[
                pltpu.VMEM((rows, width), BF16),
                pltpu.VMEM((rows, width), BF16),
                pltpu.VMEM((rows, width), F32),
                pltpu.VMEM((rows, width), BF16),
                pltpu.VMEM((rows, width), BF16),
                pltpu.VMEM((rows, width), BF16),
                pltpu.VMEM((HEADS, rows, rows), BF16),
                pltpu.VMEM((rows, width), BF16),
                pltpu.VMEM((rows, width), F32),
                pltpu.VMEM((rows, width), F32),
                pltpu.VMEM((rows, width), BF16),
                pltpu.VMEM((rows, width), BF16),
                pltpu.VMEM((rows, hidden), BF16),
                pltpu.VMEM((rows, hidden), BF16),
                pltpu.VMEM((rows, width), BF16),
                pltpu.VMEM((rows, 3 * width), BF16),
            ],
        ),
        out_shape=[
            jax.ShapeDtypeStruct(tokens.shape, BF16),
            jax.ShapeDtypeStruct(tokens.shape, BF16),
            jax.ShapeDtypeStruct((width, 3 * width), F32),
            jax.ShapeDtypeStruct((width, width), F32),
            jax.ShapeDtypeStruct((width, hidden), F32),
            jax.ShapeDtypeStruct((hidden, width), F32),
            jax.ShapeDtypeStruct((8, width), F32),
            jax.ShapeDtypeStruct((1, hidden), F32),
        ],
        compiler_params=pltpu.CompilerParams(
            dimension_semantics=("arbitrary",), vmem_limit_bytes=48 * 1024 * 1024
        ),
    )(count, tokens, cotangent, wqkv, wout, wup, wdown, small, bup)


def body(tokens, image_count, w_qkv, w_out, w_fc1, w_fc2, norm_bias, cotangent):
    slots, seq, width = tokens.shape
    shards = (w_qkv, w_out, w_fc1, w_fc2, norm_bias)
    sizes = [s.shape[0] for s in shards]
    cuts = [sum(sizes[: i + 1]) for i in range(len(sizes) - 1)]
    gathered = lax.all_gather(jnp.concatenate(shards), ("dp", "fsdp"), axis=0, tiled=False)
    parts = [p.reshape(-1) for p in jnp.split(gathered, cuts, axis=1)]
    hidden = parts[2].shape[0] // width
    wqkv = parts[0].reshape(width, 3 * width)
    wout = parts[1].reshape(width, width)
    wup = parts[2].reshape(width, hidden)
    wdown = parts[3].reshape(hidden, width)
    vec = parts[4].astype(F32)
    small = jnp.concatenate([vec[: 7 * width], vec[7 * width + hidden :]]).reshape(8, width)
    bup = vec[7 * width : 7 * width + hidden].reshape(1, hidden)
    output, grad_tokens, gqkv, gout, gup, gdown, gsmall, gbup = run_layer(
        image_count, tokens, cotangent, wqkv, wout, wup, wdown, small, bup
    )
    flat = gsmall.reshape(-1)
    gvec = jnp.concatenate([flat[: 7 * width], gbup.reshape(-1), flat[7 * width :]])
    devices = gathered.shape[0]
    terms = jnp.concatenate(
        [g.reshape(devices, -1) for g in (gqkv, gout, gup, gdown, gvec)], axis=1
    ).reshape(-1)
    summed = lax.psum_scatter(terms, ("dp", "fsdp"), scatter_dimension=0, tiled=True)
    return (output, grad_tokens, *jnp.split(summed, cuts))


def solution(mesh):
    both = P(("dp", "fsdp"))
    images = P(("dp", "fsdp"), None, None)
    return jax.shard_map(
        body,
        mesh=mesh,
        in_specs=(images, both, both, both, both, both, both, images),
        out_specs=(images, images, both, both, both, both, both),
        check_vma=False,
    )
```

```python
import functools
import math

import jax
import jax.numpy as jnp
from jax import lax
from jax.experimental import pallas as pl
from jax.experimental.pallas import tpu as pltpu
from jax.sharding import PartitionSpec as P

HEADS = 6
HEAD_DIM = 64
EPS = 1e-06
F32 = jnp.float32
BF16 = jnp.bfloat16


def mm(a, b):
    return lax.dot_general(a, b, (((1,), (0,)), ((), ())), preferred_element_type=F32)


def mm_t(a, b):
    return lax.dot_general(a, b, (((1,), (1,)), ((), ())), preferred_element_type=F32)


def t_mm(a, b):
    return lax.dot_general(a, b, (((0,), (0,)), ((), ())), preferred_element_type=F32)


def norm_parts(values, width):
    mean = jnp.sum(values, axis=-1, keepdims=True) * (1.0 / width)
    center = values - mean
    var = jnp.sum(center * center, axis=-1, keepdims=True) * (1.0 / width)
    inverse = lax.rsqrt(var + EPS)
    return center * inverse, inverse


def norm_back(upstream, normed, inverse, gain, width):
    scaled = upstream * gain
    m1 = jnp.sum(scaled, axis=-1, keepdims=True) * (1.0 / width)
    m2 = jnp.sum(scaled * normed, axis=-1, keepdims=True) * (1.0 / width)
    return inverse * (scaled - m1 - normed * m2)


def gelu_both(z):
    ez = jnp.exp(-0.5 * z * z)
    t = 1.0 / (1.0 + (0.3275911 * 0.7071067811865476) * jnp.abs(z))
    poly = ((((1.061405429 * t - 1.453152027) * t + 1.421413741) * t - 0.284496736) * t + 0.254829592) * t
    half = 0.5 * poly * ez
    cumul = jnp.where(z >= 0.0, 1.0 - half, half)
    return z * cumul, cumul + z * (ez * 0.3989422804014327)


def layer_kernel(
    count_ref, x_ref, ct_ref, wqkv_ref, wout_ref, wup_ref, wdown_ref, small_ref, bup_ref,
    out_ref, gx_ref, oqkv_ref, oout_ref, oup_ref, odown_ref, gsmall_ref, gbup_ref,
    gqkv_ref, gout_ref, gup_ref, gdown_ref,
    xs, cs, n1s, qs, ks, vs, pbs, os_, y1s, n2s, a1s, a2s, acts, dzs, dos, dqkvs,
):
    step = pl.program_id(0)
    seq, width = x_ref.shape[1], x_ref.shape[2]
    rows = xs.shape[0]
    hidden = wup_ref.shape[1]
    scale = 1.0 / math.sqrt(HEAD_DIM)

    @pl.when(step == 0)
    def _():
        xs[...] = jnp.zeros_like(xs)
        cs[...] = jnp.zeros_like(cs)
        for ref in (gqkv_ref, gout_ref, gup_ref, gdown_ref, gsmall_ref, gbup_ref):
            ref[...] = jnp.zeros_like(ref)

    live = step < count_ref[0]

    @pl.when(jnp.logical_not(live))
    def _():
        out_ref[...] = jnp.zeros_like(out_ref)
        gx_ref[...] = jnp.zeros_like(gx_ref)

    @pl.when(live)
    def _():
        xs[0:seq, :] = x_ref[0]
        cs[0:seq, :] = ct_ref[0]
        g1, c1 = small_ref[0:1, :], small_ref[1:2, :]
        bq, bv, bo = small_ref[2:3, :], small_ref[3:4, :], small_ref[4:5, :]
        g2, c2, b2 = small_ref[5:6, :], small_ref[6:7, :], small_ref[7:8, :]
        n1, inv1 = norm_parts(xs[...].astype(F32), width)
        n1s[...] = n1
        a1s[...] = (n1 * g1 + c1).astype(BF16)
        qs[...] = (mm(a1s[...], wqkv_ref[:, :width]) + bq).astype(BF16)
        ks[...] = mm(a1s[...], wqkv_ref[:, width : 2 * width]).astype(BF16)
        vs[...] = (mm(a1s[...], wqkv_ref[:, 2 * width :]) + bv).astype(BF16)
        lane = lax.broadcasted_iota(jnp.int32, (rows, 2 * HEAD_DIM), 1)
        halves = (lane < HEAD_DIM, lane >= HEAD_DIM)
        keyrow = lax.broadcasted_iota(jnp.int32, (rows, rows), 0)
        zero = jnp.zeros((rows, 2 * HEAD_DIM), BF16)
        for pair in range(HEADS // 2):
            cols = slice(pair * 2 * HEAD_DIM, (pair + 1) * 2 * HEAD_DIM)
            qp, kp, vp = qs[:, cols], ks[:, cols], vs[:, cols]
            both = None
            for h in range(2):
                km = jnp.where(halves[h], kp, zero)
                vm = jnp.where(halves[h], vp, zero)
                scores = mm_t(km, qp) * scale
                scores = jnp.where(keyrow < seq, scores, -1e30)
                top = jnp.max(scores, axis=0, keepdims=True)
                expo = jnp.exp(scores - top)
                total = jnp.sum(expo, axis=0, keepdims=True)
                prob = expo * (1.0 / total)
                pbs[pair * 2 + h] = prob.astype(BF16)
                part = t_mm(pbs[pair * 2 + h], vm)
                both = part if both is None else both + part
            os_[:, cols] = both.astype(BF16)
        y1 = xs[...].astype(F32) + (mm(os_[...], wout_ref[...]) + bo)
        y1s[...] = y1
        n2, inv2 = norm_parts(y1, width)
        n2s[...] = n2
        a2s[...] = (n2 * g2 + c2).astype(BF16)
        tile = 256
        for j in range(hidden // tile):
            cols = slice(j * tile, (j + 1) * tile)
            z = mm(a2s[...], wup_ref[:, cols]) + bup_ref[:, cols]
            act, slope = gelu_both(z)
            acts[:, cols] = act.astype(BF16)
            dz = (mm_t(cs[...], wdown_ref[cols, :]) * slope).astype(BF16)
            dzs[:, cols] = dz
            gbup_ref[:, cols] += jnp.sum(dz.astype(F32), axis=0, keepdims=True)
        y = y1s[...] + mm(acts[...], wdown_ref[...]) + b2
        out_ref[0] = y[:seq].astype(BF16)
        gdown_ref[...] += t_mm(acts[...], cs[...])
        gup_ref[...] += t_mm(a2s[...], dzs[...])
        da2 = mm_t(dzs[...], wup_ref[...])
        ct = cs[...].astype(F32)
        n2 = n2s[...]
        gsmall_ref[7:8, :] += jnp.sum(ct, axis=0, keepdims=True)
        gsmall_ref[5:6, :] += jnp.sum(da2 * n2, axis=0, keepdims=True)
        gsmall_ref[6:7, :] += jnp.sum(da2, axis=0, keepdims=True)
        dy1 = ct + norm_back(da2, n2, inv2, g2, width)
        y1s[...] = dy1
        da = dy1.astype(BF16)
        gsmall_ref[4:5, :] += jnp.sum(da.astype(F32), axis=0, keepdims=True)
        gout_ref[...] += t_mm(os_[...], da)
        dos[...] = mm_t(da, wout_ref[...]).astype(BF16)
        for pair in range(HEADS // 2):
            cols = slice(pair * 2 * HEAD_DIM, (pair + 1) * 2 * HEAD_DIM)
            qp, kp, vp, dop = qs[:, cols], ks[:, cols], vs[:, cols], dos[:, cols]
            dq = dk = dv = None
            for h in range(2):
                qm = jnp.where(halves[h], qp, zero)
                km = jnp.where(halves[h], kp, zero)
                vm = jnp.where(halves[h], vp, zero)
                dom = jnp.where(halves[h], dop, zero)
                pb = pbs[pair * 2 + h]
                prob = pb.astype(F32)
                dp = mm_t(vm, dop)
                inner = jnp.sum(prob * dp, axis=0, keepdims=True)
                ds = (prob * (dp - inner)).astype(BF16)
                dv_h = mm(pb, dom)
                dk_h = mm(ds, qm)
                dq_h = t_mm(ds, km)
                dq = dq_h if dq is None else dq + dq_h
                dk = dk_h if dk is None else dk + dk_h
                dv = dv_h if dv is None else dv + dv_h
            base = pair * 2 * HEAD_DIM
            dqkvs[:, base : base + 2 * HEAD_DIM] = (dq * scale).astype(BF16)
            dqkvs[:, width + base : width + base + 2 * HEAD_DIM] = (dk * scale).astype(BF16)
            dqkvs[:, 2 * width + base : 2 * width + base + 2 * HEAD_DIM] = dv.astype(BF16)
        gsmall_ref[2:3, :] += jnp.sum(dqkvs[:, :width].astype(F32), axis=0, keepdims=True)
        gsmall_ref[3:4, :] += jnp.sum(dqkvs[:, 2 * width :].astype(F32), axis=0, keepdims=True)
        gqkv_ref[...] += t_mm(a1s[...], dqkvs[...])
        da1 = mm_t(dqkvs[...], wqkv_ref[...])
        n1 = n1s[...]
        gsmall_ref[0:1, :] += jnp.sum(da1 * n1, axis=0, keepdims=True)
        gsmall_ref[1:2, :] += jnp.sum(da1, axis=0, keepdims=True)
        gx = y1s[...] + norm_back(da1, n1, inv1, g1, width)
        gx_ref[0] = gx[:seq].astype(BF16)

    @pl.when(step == pl.num_programs(0) - 1)
    def _():
        oqkv_ref[...] = gqkv_ref[...].astype(BF16)
        oout_ref[...] = gout_ref[...].astype(BF16)
        oup_ref[...] = gup_ref[...].astype(BF16)
        odown_ref[...] = gdown_ref[...].astype(BF16)


def run_layer(count, tokens, cotangent, wqkv, wout, wup, wdown, small, bup):
    slots, seq, width = tokens.shape
    hidden = wup.shape[1]
    rows = (seq + 15) // 16 * 16

    def whole(shape):
        return pl.BlockSpec(shape, lambda i, c: (0,) * len(shape), pipeline_mode=pl.Buffered(1))

    def image():
        return pl.BlockSpec((1, seq, width), lambda i, c: (i, 0, 0))

    return pl.pallas_call(
        layer_kernel,
        grid_spec=pltpu.PrefetchScalarGridSpec(
            num_scalar_prefetch=1,
            grid=(slots,),
            in_specs=[
                image(), image(),
                whole((width, 3 * width)), whole((width, width)), whole((width, hidden)),
                whole((hidden, width)), whole((8, width)), whole((1, hidden)),
            ],
            out_specs=[
                image(), image(),
                whole((width, 3 * width)), whole((width, width)), whole((width, hidden)),
                whole((hidden, width)), whole((8, width)), whole((1, hidden)),
            ],
            scratch_shapes=[
                pltpu.VMEM((width, 3 * width), F32),
                pltpu.VMEM((width, width), F32),
                pltpu.VMEM((width, hidden), F32),
                pltpu.VMEM((hidden, width), F32),
                pltpu.VMEM((rows, width), BF16),
                pltpu.VMEM((rows, width), BF16),
                pltpu.VMEM((rows, width), F32),
                pltpu.VMEM((rows, width), BF16),
                pltpu.VMEM((rows, width), BF16),
                pltpu.VMEM((rows, width), BF16),
                pltpu.VMEM((HEADS, rows, rows), BF16),
                pltpu.VMEM((rows, width), BF16),
                pltpu.VMEM((rows, width), F32),
                pltpu.VMEM((rows, width), F32),
                pltpu.VMEM((rows, width), BF16),
                pltpu.VMEM((rows, width), BF16),
                pltpu.VMEM((rows, hidden), BF16),
                pltpu.VMEM((rows, hidden), BF16),
                pltpu.VMEM((rows, width), BF16),
                pltpu.VMEM((rows, 3 * width), BF16),
            ],
        ),
        out_shape=[
            jax.ShapeDtypeStruct(tokens.shape, BF16),
            jax.ShapeDtypeStruct(tokens.shape, BF16),
            jax.ShapeDtypeStruct((width, 3 * width), BF16),
            jax.ShapeDtypeStruct((width, width), BF16),
            jax.ShapeDtypeStruct((width, hidden), BF16),
            jax.ShapeDtypeStruct((hidden, width), BF16),
            jax.ShapeDtypeStruct((8, width), F32),
            jax.ShapeDtypeStruct((1, hidden), F32),
        ],
        compiler_params=pltpu.CompilerParams(
            dimension_semantics=("arbitrary",), vmem_limit_bytes=48 * 1024 * 1024
        ),
    )(count, tokens, cotangent, wqkv, wout, wup, wdown, small, bup)


MESH = pl.DeviceIdType.MESH
CORES = 2
LANES = 128


def greet(n_dp, n_y, dp, y, core):
    barrier = pltpu.get_barrier_semaphore()
    pl.semaphore_signal(
        barrier, inc=1, device_id=(dp, y * CORES + 1 - core), device_id_type=MESH
    )
    for k in range(1, n_y):
        other = lax.rem(y + k, n_y)
        pl.semaphore_signal(barrier, inc=1, device_id=(dp, other * CORES + core), device_id_type=MESH)
    for k in range(1, n_dp):
        other = lax.rem(dp + k, n_dp)
        pl.semaphore_signal(barrier, inc=1, device_id=(other, y * CORES + core), device_id_type=MESH)
    pl.semaphore_wait(barrier, n_dp + n_y - 1)


def gather_kernel(n_dp, n_y, count, *refs):
    parts, (o_ref, x_ref, own_sem, dp_send, y_send, core_send, recv_sem) = refs[:count], refs[count:]
    fill(x_ref, parts)
    dp = lax.axis_index("dp")
    place = lax.axis_index("fsdp")
    y, core = place // CORES, lax.rem(place, CORES)
    n_f = n_y * CORES
    greet(n_dp, n_y, dp, y, core)
    me = dp * n_f + place
    sent = []

    def send(src, slot, sem, device):
        copy = pltpu.make_async_remote_copy(
            src_ref=src, dst_ref=o_ref.at[slot], send_sem=sem, recv_sem=recv_sem.at[slot],
            device_id=device, device_id_type=MESH,
        )
        copy.start()
        sent.append(copy)

    def arrived(slot):
        pltpu.make_async_remote_copy(
            src_ref=x_ref, dst_ref=o_ref.at[slot], send_sem=own_sem, recv_sem=recv_sem.at[slot],
            device_id=(dp, y * CORES + 1 - core), device_id_type=MESH,
        ).wait_recv()

    own = pltpu.make_async_copy(x_ref, o_ref.at[me], own_sem)
    own.start()
    for k in range(1, n_dp):
        send(x_ref, me, dp_send.at[k], (lax.rem(dp + k, n_dp), place))
    for j in range(n_dp):
        slot = lax.rem(dp + n_dp - j, n_dp) * n_f + place
        if j:
            arrived(slot)
        src = o_ref.at[slot] if j else x_ref
        for k in range(1, n_y):
            send(src, slot, y_send.at[j, k], (dp, lax.rem(y + k, n_y) * CORES + core))
        send(src, slot, core_send.at[j, 0], (dp, y * CORES + 1 - core))
    for j in range(n_dp):
        for k in range(1, n_y):
            slot = lax.rem(dp + n_dp - j, n_dp) * n_f + lax.rem(y + n_y - k, n_y) * CORES + core
            arrived(slot)
            send(o_ref.at[slot], slot, core_send.at[j, k], (dp, y * CORES + 1 - core))
    for j in range(n_dp):
        for k in range(n_y):
            slot = lax.rem(dp + n_dp - j, n_dp) * n_f + lax.rem(y + n_y - k, n_y) * CORES + 1 - core
            arrived(slot)
    own.wait()
    for copy in sent:
        copy.wait_send()


def fill(block, parts):
    at = 0
    for part in parts:
        block[at : at + part.shape[0], :] = part[...]
        at += tall(part.shape[0])


def gather_all(parts, n_dp, n_f):
    n_y = n_f // CORES
    height = sum(tall(p.shape[0]) for p in parts)
    block = (height, LANES)
    return pl.pallas_call(
        lambda *refs: gather_kernel(n_dp, n_y, len(parts), *refs),
        out_shape=jax.ShapeDtypeStruct((n_dp * n_f, *block), BF16),
        in_specs=[pl.BlockSpec(memory_space=pltpu.VMEM)] * len(parts),
        out_specs=pl.BlockSpec(memory_space=pl.ANY),
        scratch_shapes=[
            pltpu.VMEM(block, BF16),
            pltpu.SemaphoreType.DMA,
            pltpu.SemaphoreType.DMA((n_dp,)),
            pltpu.SemaphoreType.DMA((n_dp, n_y)),
            pltpu.SemaphoreType.DMA((n_dp, n_y)),
            pltpu.SemaphoreType.DMA((n_dp * n_f,)),
        ],
        compiler_params=pltpu.CompilerParams(collective_id=0, has_side_effects=True),
    )(*parts)


def scatter_kernel(n_dp, n_y, count, *refs):
    parts, outs = refs[:count], refs[count : 2 * count]
    g_ref, o_ref, r1, a1, r2, a2, r3, s1, s2, s3, q1, q2, q3 = refs[2 * count :]

    def fill_slot(slot, carry):
        at = 0
        for part in parts:
            g_ref[slot, at : at + part.shape[1], :] = part[slot]
            at += tall(part.shape[1])
        return carry

    lax.fori_loop(0, n_dp * n_y * CORES, fill_slot, 0)
    dp = lax.axis_index("dp")
    place = lax.axis_index("fsdp")
    y, core = place // CORES, lax.rem(place, CORES)
    n_f = n_y * CORES
    greet(n_dp, n_y, dp, y, core)
    sibling = (dp, y * CORES + 1 - core)
    sent = []

    def send(src, dst, ssem, rsem, device):
        copy = pltpu.make_async_remote_copy(
            src_ref=src, dst_ref=dst, send_sem=ssem, recv_sem=rsem,
            device_id=device, device_id_type=MESH,
        )
        copy.start()
        sent.append(copy)

    def arrived(dst, rsem):
        pltpu.make_async_remote_copy(
            src_ref=dst, dst_ref=dst, send_sem=s1.at[0, 0], recv_sem=rsem,
            device_id=sibling, device_id_type=MESH,
        ).wait_recv()

    order = list(range(1, n_dp)) + [0]
    hops = list(range(1, n_y)) + [0]

    def target(j):
        return lax.rem(dp + j, n_dp)

    def column(k):
        return lax.rem(y + k, n_y)

    for k in hops:
        for j in order:
            slot = target(j) * n_f + column(k) * CORES + 1 - core
            send(g_ref.at[slot], r1.at[j, k], s1.at[j, k], q1.at[j, k], sibling)
    for k in hops[:-1]:
        for j in order:
            arrived(r1.at[j, k], q1.at[j, k])
            slot = target(j) * n_f + column(k) * CORES + core
            a1[j, k - 1] = (g_ref[slot].astype(F32) + r1[j, k].astype(F32)).astype(BF16)
            send(a1.at[j, k - 1], r2.at[j, k - 1], s2.at[j, k - 1], q2.at[j, k - 1],
                 (dp, column(k) * CORES + core))
    for j in order:
        arrived(r1.at[j, 0], q1.at[j, 0])
        slot = target(j) * n_f + place
        total = g_ref[slot].astype(F32) + r1[j, 0].astype(F32)
        for k in hops[:-1]:
            arrived(r2.at[j, k - 1], q2.at[j, k - 1])
            total = total + r2[j, k - 1].astype(F32)
        if j:
            a2[j - 1] = total.astype(BF16)
            send(a2.at[j - 1], r3.at[j - 1], s3.at[j - 1], q3.at[j - 1], (target(j), place))
        else:
            o_ref[...] = total
    for j in order[:-1]:
        arrived(r3.at[j - 1], q3.at[j - 1])
        o_ref[...] += r3[j - 1].astype(F32)
    at = 0
    for out in outs:
        out[...] = o_ref[at : at + out.shape[0], :]
        at += tall(out.shape[0])
    for copy in sent:
        copy.wait_send()


def scatter_sum(terms, n_dp, n_f):
    n_y = n_f // CORES
    block = (sum(tall(t.shape[1]) for t in terms), LANES)
    far = max(n_y - 1, 1)
    dma = pltpu.SemaphoreType.DMA
    return pl.pallas_call(
        lambda *refs: scatter_kernel(n_dp, n_y, len(terms), *refs),
        out_shape=[jax.ShapeDtypeStruct(t.shape[1:], F32) for t in terms],
        in_specs=[pl.BlockSpec(memory_space=pltpu.VMEM)] * len(terms),
        out_specs=[pl.BlockSpec(memory_space=pltpu.VMEM)] * len(terms),
        scratch_shapes=[
            pltpu.VMEM((n_dp * n_f, *block), BF16),
            pltpu.VMEM(block, F32),
            pltpu.VMEM((n_dp, n_y, *block), BF16),
            pltpu.VMEM((n_dp, far, *block), BF16),
            pltpu.VMEM((n_dp, far, *block), BF16),
            pltpu.VMEM((n_dp - 1, *block), BF16),
            pltpu.VMEM((n_dp - 1, *block), BF16),
            dma((n_dp, n_y)), dma((n_dp, far)), dma((n_dp - 1,)),
            dma((n_dp, n_y)), dma((n_dp, far)), dma((n_dp - 1,)),
        ],
        compiler_params=pltpu.CompilerParams(
            collective_id=1, has_side_effects=True, vmem_limit_bytes=40 * 1024 * 1024
        ),
    )(*terms)


def lanes_of(size):
    return (size + LANES - 1) // LANES


def to_rows(values, count):
    flat = values.reshape(count, -1)
    size = flat.shape[1]
    if size % LANES:
        flat = jnp.pad(flat, ((0, 0), (0, lanes_of(size) * LANES - size)))
    else:
        flat = values
    return flat.reshape(count, lanes_of(size), LANES)


def tall(height):
    return (height + 15) // 16 * 16


def unpack(rows, sizes):
    outs, at = [], 0
    for size in sizes:
        height = lanes_of(size)
        piece = rows[:, at : at + height]
        if size % LANES:
            piece = piece.reshape(rows.shape[0], height * LANES)[:, :size]
        outs.append(piece)
        at += tall(height)
    return outs


def body(n_dp, n_f, tokens, image_count, w_qkv, w_out, w_fc1, w_fc2, norm_bias, cotangent):
    slots, seq, width = tokens.shape
    shards = (w_qkv, w_out, w_fc1, w_fc2, norm_bias)
    sizes = [s.shape[0] for s in shards]
    devices = n_dp * n_f
    gathered = gather_all([to_rows(p, 1)[0] for p in shards], n_dp, n_f)
    parts = unpack(gathered, sizes)
    hidden = sizes[2] * devices // width
    wqkv = parts[0].reshape(width, 3 * width)
    wout = parts[1].reshape(width, width)
    wup = parts[2].reshape(width, hidden)
    wdown = parts[3].reshape(hidden, width)
    vec = parts[4].astype(F32).reshape(-1)
    small = jnp.concatenate([vec[: 7 * width], vec[7 * width + hidden :]]).reshape(8, width)
    bup = vec[7 * width : 7 * width + hidden].reshape(1, hidden)
    output, grad_tokens, gqkv, gout, gup, gdown, gsmall, gbup = run_layer(
        image_count, tokens, cotangent, wqkv, wout, wup, wdown, small, bup
    )
    flat = gsmall.reshape(-1)
    gvec = jnp.concatenate([flat[: 7 * width], gbup.reshape(-1), flat[7 * width :]]).astype(BF16)
    terms = [to_rows(g, devices) for g in (gqkv, gout, gup, gdown, gvec)]
    summed = scatter_sum(terms, n_dp, n_f)
    grads = [g.reshape(-1)[:size] for g, size in zip(summed, sizes)]
    return (output, grad_tokens, *grads)


def solution(mesh):
    both = P(("dp", "fsdp"))
    images = P(("dp", "fsdp"), None, None)
    sizes = (mesh.shape["dp"], mesh.shape["fsdp"])
    return jax.shard_map(
        functools.partial(body, *sizes),
        mesh=mesh,
        in_specs=(images, both, both, both, both, both, both, images),
        out_specs=(images, images, both, both, both, both, both),
        check_vma=False,
    )
```

```python
import functools
import math

import jax
import jax.numpy as jnp
from jax import lax
from jax.experimental import pallas as pl
from jax.experimental.pallas import tpu as pltpu
from jax.sharding import PartitionSpec as P

HEADS = 6
HEAD_DIM = 64
EPS = 1e-06
F32 = jnp.float32
BF16 = jnp.bfloat16


def mm(a, b):
    return lax.dot_general(a, b, (((1,), (0,)), ((), ())), preferred_element_type=F32)


def mm_t(a, b):
    return lax.dot_general(a, b, (((1,), (1,)), ((), ())), preferred_element_type=F32)


def t_mm(a, b):
    return lax.dot_general(a, b, (((0,), (0,)), ((), ())), preferred_element_type=F32)


def norm_parts(values, width):
    mean = jnp.sum(values, axis=-1, keepdims=True) * (1.0 / width)
    center = values - mean
    var = jnp.sum(center * center, axis=-1, keepdims=True) * (1.0 / width)
    inverse = lax.rsqrt(var + EPS)
    return center * inverse, inverse


def norm_back(upstream, normed, inverse, gain, width):
    scaled = upstream * gain
    m1 = jnp.sum(scaled, axis=-1, keepdims=True) * (1.0 / width)
    m2 = jnp.sum(scaled * normed, axis=-1, keepdims=True) * (1.0 / width)
    return inverse * (scaled - m1 - normed * m2)


def gelu_both(z):
    ez = jnp.exp2(z * z * (-0.5 * 1.4426950408889634))
    d = 1.0 + (0.3275911 * 0.7071067811865476) * jnp.abs(z)
    t = pl.reciprocal(d, approx=True)
    t = t * (2.0 - d * t)
    poly = (((0.5307027145 * t - 0.7265760135) * t + 0.7107068705) * t - 0.142248368) * t + 0.127414796
    half = poly * t * ez
    cumul = jnp.where(z >= 0.0, 1.0 - half, half)
    return z * cumul, cumul + z * (ez * 0.3989422804014327)


def layer_kernel(
    count_ref, x_ref, ct_ref, wqkv_ref, wout_ref, wup_ref, wdown_ref, small_ref, bup_ref,
    out_ref, gx_ref, oqkv_ref, oout_ref, oup_ref, odown_ref, gsmall_ref, gbup_ref,
    gqkv_ref, gout_ref, gup_ref, gdown_ref,
    xs, cs, n1s, qs, ks, vs, pbs, os_, y1s, n2s, a1s, a2s, acts, dzs, dos, dqkvs,
):
    step = pl.program_id(0)
    seq, width = x_ref.shape[1], x_ref.shape[2]
    rows = xs.shape[0]
    hidden = wup_ref.shape[1]
    scale = 1.0 / math.sqrt(HEAD_DIM)

    @pl.when(step == 0)
    def _():
        xs[...] = jnp.zeros_like(xs)
        cs[...] = jnp.zeros_like(cs)
        for ref in (gqkv_ref, gout_ref, gup_ref, gdown_ref, gsmall_ref, gbup_ref):
            ref[...] = jnp.zeros_like(ref)

    live = step < count_ref[0]

    @pl.when(jnp.logical_not(live))
    def _():
        out_ref[...] = jnp.zeros_like(out_ref)
        gx_ref[...] = jnp.zeros_like(gx_ref)

    @pl.when(live)
    def _():
        xs[0:seq, :] = x_ref[0]
        cs[0:seq, :] = ct_ref[0]
        g1, c1 = small_ref[0:1, :], small_ref[1:2, :]
        bq, bv, bo = small_ref[2:3, :], small_ref[3:4, :], small_ref[4:5, :]
        g2, c2, b2 = small_ref[5:6, :], small_ref[6:7, :], small_ref[7:8, :]
        n1, inv1 = norm_parts(xs[...].astype(F32), width)
        n1s[...] = n1
        a1s[...] = (n1 * g1 + c1).astype(BF16)
        qs[...] = ((mm(a1s[...], wqkv_ref[:, :width]) + bq).astype(BF16).astype(F32) * scale).astype(BF16)
        ks[...] = mm(a1s[...], wqkv_ref[:, width : 2 * width]).astype(BF16)
        vs[...] = (mm(a1s[...], wqkv_ref[:, 2 * width :]) + bv).astype(BF16)
        lane = lax.broadcasted_iota(jnp.int32, (rows, 2 * HEAD_DIM), 1)
        halves = (lane < HEAD_DIM, lane >= HEAD_DIM)
        whole_rows = seq // 8 * 8
        keyrow = whole_rows + lax.broadcasted_iota(jnp.int32, (rows - whole_rows, rows), 0)
        zero = jnp.zeros((rows, 2 * HEAD_DIM), BF16)
        for pair in range(HEADS // 2):
            cols = slice(pair * 2 * HEAD_DIM, (pair + 1) * 2 * HEAD_DIM)
            qp, kp, vp = qs[:, cols], ks[:, cols], vs[:, cols]
            both = None
            for h in range(2):
                km = jnp.where(halves[h], kp, zero)
                vm = jnp.where(halves[h], vp, zero)
                scores = mm_t(km, qp)
                scores = jnp.concatenate(
                    [scores[:whole_rows], jnp.where(keyrow < seq, scores[whole_rows:], -1e30)], axis=0
                )
                top = jnp.max(scores, axis=0, keepdims=True)
                expo = jnp.exp(scores - top)
                total = jnp.sum(expo, axis=0, keepdims=True)
                prob = expo * (1.0 / total)
                pbs[pair * 2 + h] = prob.astype(BF16)
                part = t_mm(pbs[pair * 2 + h], vm)
                both = part if both is None else both + part
            os_[:, cols] = both.astype(BF16)
        y1 = xs[...].astype(F32) + (mm(os_[...], wout_ref[...]) + bo)
        y1s[...] = y1
        n2, inv2 = norm_parts(y1, width)
        n2s[...] = n2
        a2s[...] = (n2 * g2 + c2).astype(BF16)
        tile = 256
        for j in range(hidden // tile):
            cols = slice(j * tile, (j + 1) * tile)
            z = mm(a2s[...], wup_ref[:, cols]) + bup_ref[:, cols]
            act, slope = gelu_both(z)
            acts[:, cols] = act.astype(BF16)
            dz = (mm_t(cs[...], wdown_ref[cols, :]) * slope).astype(BF16)
            dzs[:, cols] = dz
            gbup_ref[:, cols] += jnp.sum(dz.astype(F32), axis=0, keepdims=True)
        y = y1s[...] + mm(acts[...], wdown_ref[...]) + b2
        out_ref[0] = y[:seq].astype(BF16)
        gdown_ref[...] += t_mm(cs[...], acts[...])
        gup_ref[...] += t_mm(a2s[...], dzs[...])
        da2 = mm_t(dzs[...], wup_ref[...])
        ct = cs[...].astype(F32)
        n2 = n2s[...]
        gsmall_ref[7:8, :] += jnp.sum(ct, axis=0, keepdims=True)
        gsmall_ref[5:6, :] += jnp.sum(da2 * n2, axis=0, keepdims=True)
        gsmall_ref[6:7, :] += jnp.sum(da2, axis=0, keepdims=True)
        dy1 = ct + norm_back(da2, n2, inv2, g2, width)
        y1s[...] = dy1
        da = dy1.astype(BF16)
        gsmall_ref[4:5, :] += jnp.sum(da.astype(F32), axis=0, keepdims=True)
        gout_ref[...] += t_mm(os_[...], da)
        dos[...] = mm_t(da, wout_ref[...]).astype(BF16)
        for pair in range(HEADS // 2):
            cols = slice(pair * 2 * HEAD_DIM, (pair + 1) * 2 * HEAD_DIM)
            qp, kp, vp, dop = qs[:, cols], ks[:, cols], vs[:, cols], dos[:, cols]
            dq = dk = dv = None
            for h in range(2):
                qm = jnp.where(halves[h], qp, zero)
                km = jnp.where(halves[h], kp, zero)
                vm = jnp.where(halves[h], vp, zero)
                dom = jnp.where(halves[h], dop, zero)
                pb = pbs[pair * 2 + h]
                prob = pb.astype(F32)
                dp = mm_t(vm, dop)
                inner = jnp.sum(prob * dp, axis=0, keepdims=True)
                ds = (prob * (dp - inner)).astype(BF16)
                dv_h = mm(pb, dom)
                dk_h = mm(ds, qm)
                dq_h = t_mm(ds, km)
                dq = dq_h if dq is None else dq + dq_h
                dk = dk_h if dk is None else dk + dk_h
                dv = dv_h if dv is None else dv + dv_h
            base = pair * 2 * HEAD_DIM
            dqkvs[:, base : base + 2 * HEAD_DIM] = (dq * scale).astype(BF16)
            dqkvs[:, width + base : width + base + 2 * HEAD_DIM] = dk.astype(BF16)
            dqkvs[:, 2 * width + base : 2 * width + base + 2 * HEAD_DIM] = dv.astype(BF16)
        gsmall_ref[2:3, :] += jnp.sum(dqkvs[:, :width].astype(F32), axis=0, keepdims=True)
        gsmall_ref[3:4, :] += jnp.sum(dqkvs[:, 2 * width :].astype(F32), axis=0, keepdims=True)
        gqkv_ref[...] += t_mm(a1s[...], dqkvs[...])
        da1 = mm_t(dqkvs[...], wqkv_ref[...])
        n1 = n1s[...]
        gsmall_ref[0:1, :] += jnp.sum(da1 * n1, axis=0, keepdims=True)
        gsmall_ref[1:2, :] += jnp.sum(da1, axis=0, keepdims=True)
        gx = y1s[...] + norm_back(da1, n1, inv1, g1, width)
        gx_ref[0] = gx[:seq].astype(BF16)

    @pl.when(step == pl.num_programs(0) - 1)
    def _():
        oqkv_ref[...] = gqkv_ref[...].astype(BF16)
        oout_ref[...] = gout_ref[...].astype(BF16)
        oup_ref[...] = gup_ref[...].astype(BF16)
        for j in range(hidden // width):
            block = slice(j * width, (j + 1) * width)
            odown_ref[block, :] = gdown_ref[:, block].T.astype(BF16)


def run_layer(count, tokens, cotangent, wqkv, wout, wup, wdown, small, bup):
    slots, seq, width = tokens.shape
    hidden = wup.shape[1]
    rows = (seq + 15) // 16 * 16

    def whole(shape):
        return pl.BlockSpec(shape, lambda i, c: (0,) * len(shape), pipeline_mode=pl.Buffered(1))

    def image():
        return pl.BlockSpec((1, seq, width), lambda i, c: (i, 0, 0))

    return pl.pallas_call(
        layer_kernel,
        grid_spec=pltpu.PrefetchScalarGridSpec(
            num_scalar_prefetch=1,
            grid=(slots,),
            in_specs=[
                image(), image(),
                whole((width, 3 * width)), whole((width, width)), whole((width, hidden)),
                whole((hidden, width)), whole((8, width)), whole((1, hidden)),
            ],
            out_specs=[
                image(), image(),
                whole((width, 3 * width)), whole((width, width)), whole((width, hidden)),
                whole((hidden, width)), whole((8, width)), whole((1, hidden)),
            ],
            scratch_shapes=[
                pltpu.VMEM((width, 3 * width), F32),
                pltpu.VMEM((width, width), F32),
                pltpu.VMEM((width, hidden), F32),
                pltpu.VMEM((width, hidden), F32),
                pltpu.VMEM((rows, width), BF16),
                pltpu.VMEM((rows, width), BF16),
                pltpu.VMEM((rows, width), F32),
                pltpu.VMEM((rows, width), BF16),
                pltpu.VMEM((rows, width), BF16),
                pltpu.VMEM((rows, width), BF16),
                pltpu.VMEM((HEADS, rows, rows), BF16),
                pltpu.VMEM((rows, width), BF16),
                pltpu.VMEM((rows, width), F32),
                pltpu.VMEM((rows, width), F32),
                pltpu.VMEM((rows, width), BF16),
                pltpu.VMEM((rows, width), BF16),
                pltpu.VMEM((rows, hidden), BF16),
                pltpu.VMEM((rows, hidden), BF16),
                pltpu.VMEM((rows, width), BF16),
                pltpu.VMEM((rows, 3 * width), BF16),
            ],
        ),
        out_shape=[
            jax.ShapeDtypeStruct(tokens.shape, BF16),
            jax.ShapeDtypeStruct(tokens.shape, BF16),
            jax.ShapeDtypeStruct((width, 3 * width), BF16),
            jax.ShapeDtypeStruct((width, width), BF16),
            jax.ShapeDtypeStruct((width, hidden), BF16),
            jax.ShapeDtypeStruct((hidden, width), BF16),
            jax.ShapeDtypeStruct((8, width), F32),
            jax.ShapeDtypeStruct((1, hidden), F32),
        ],
        compiler_params=pltpu.CompilerParams(
            dimension_semantics=("arbitrary",), vmem_limit_bytes=48 * 1024 * 1024
        ),
    )(count, tokens, cotangent, wqkv, wout, wup, wdown, small, bup)


MESH = pl.DeviceIdType.MESH
CORES = 2
LANES = 128


def greet(n_dp, n_y, dp, y, core):
    barrier = pltpu.get_barrier_semaphore()
    pl.semaphore_signal(
        barrier, inc=1, device_id=(dp, y * CORES + 1 - core), device_id_type=MESH
    )
    for k in range(1, n_y):
        other = lax.rem(y + k, n_y)
        pl.semaphore_signal(barrier, inc=1, device_id=(dp, other * CORES + core), device_id_type=MESH)
    for k in range(1, n_dp):
        other = lax.rem(dp + k, n_dp)
        pl.semaphore_signal(barrier, inc=1, device_id=(other, y * CORES + core), device_id_type=MESH)
    pl.semaphore_wait(barrier, n_dp + n_y - 1)


def gather_kernel(n_dp, n_y, count, *refs):
    parts, (o_ref, x_ref, own_sem, dp_send, y_send, core_send, recv_sem) = refs[:count], refs[count:]
    fill(x_ref, parts)
    dp = lax.axis_index("dp")
    place = lax.axis_index("fsdp")
    y, core = place // CORES, lax.rem(place, CORES)
    n_f = n_y * CORES
    greet(n_dp, n_y, dp, y, core)
    me = dp * n_f + place
    sent = []

    def send(src, slot, sem, device):
        copy = pltpu.make_async_remote_copy(
            src_ref=src, dst_ref=o_ref.at[slot], send_sem=sem, recv_sem=recv_sem.at[slot],
            device_id=device, device_id_type=MESH,
        )
        copy.start()
        sent.append(copy)

    def arrived(slot):
        pltpu.make_async_remote_copy(
            src_ref=x_ref, dst_ref=o_ref.at[slot], send_sem=own_sem, recv_sem=recv_sem.at[slot],
            device_id=(dp, y * CORES + 1 - core), device_id_type=MESH,
        ).wait_recv()

    own = pltpu.make_async_copy(x_ref, o_ref.at[me], own_sem)
    own.start()
    for k in range(1, n_dp):
        send(x_ref, me, dp_send.at[k], (lax.rem(dp + k, n_dp), place))
    for j in range(n_dp):
        slot = lax.rem(dp + n_dp - j, n_dp) * n_f + place
        if j:
            arrived(slot)
        src = o_ref.at[slot] if j else x_ref
        for k in range(1, n_y):
            send(src, slot, y_send.at[j, k], (dp, lax.rem(y + k, n_y) * CORES + core))
        send(src, slot, core_send.at[j, 0], (dp, y * CORES + 1 - core))
    for j in range(n_dp):
        for k in range(1, n_y):
            slot = lax.rem(dp + n_dp - j, n_dp) * n_f + lax.rem(y + n_y - k, n_y) * CORES + core
            arrived(slot)
            send(o_ref.at[slot], slot, core_send.at[j, k], (dp, y * CORES + 1 - core))
    for j in range(n_dp):
        for k in range(n_y):
            slot = lax.rem(dp + n_dp - j, n_dp) * n_f + lax.rem(y + n_y - k, n_y) * CORES + 1 - core
            arrived(slot)
    own.wait()
    for copy in sent:
        copy.wait_send()


def fill(block, parts):
    at = 0
    for part in parts:
        block[at : at + part.shape[0], :] = part[...]
        at += tall(part.shape[0])


def gather_all(parts, n_dp, n_f):
    n_y = n_f // CORES
    height = sum(tall(p.shape[0]) for p in parts)
    block = (height, LANES)
    return pl.pallas_call(
        lambda *refs: gather_kernel(n_dp, n_y, len(parts), *refs),
        out_shape=jax.ShapeDtypeStruct((n_dp * n_f, *block), BF16),
        in_specs=[pl.BlockSpec(memory_space=pltpu.VMEM)] * len(parts),
        out_specs=pl.BlockSpec(memory_space=pl.ANY),
        scratch_shapes=[
            pltpu.VMEM(block, BF16),
            pltpu.SemaphoreType.DMA,
            pltpu.SemaphoreType.DMA((n_dp,)),
            pltpu.SemaphoreType.DMA((n_dp, n_y)),
            pltpu.SemaphoreType.DMA((n_dp, n_y)),
            pltpu.SemaphoreType.DMA((n_dp * n_f,)),
        ],
        compiler_params=pltpu.CompilerParams(collective_id=0, has_side_effects=True),
    )(*parts)


def scatter_kernel(n_dp, n_y, count, *refs):
    parts, outs = refs[:count], refs[count : 2 * count]
    g_ref, o_ref, r1, a1, r2, a2, r3, s1, s2, s3, q1, q2, q3 = refs[2 * count :]

    def fill_slot(slot, carry):
        at = 0
        for part in parts:
            g_ref[slot, at : at + part.shape[1], :] = part[slot]
            at += tall(part.shape[1])
        return carry

    lax.fori_loop(0, n_dp * n_y * CORES, fill_slot, 0)
    dp = lax.axis_index("dp")
    place = lax.axis_index("fsdp")
    y, core = place // CORES, lax.rem(place, CORES)
    n_f = n_y * CORES
    greet(n_dp, n_y, dp, y, core)
    sibling = (dp, y * CORES + 1 - core)
    sent = []

    def send(src, dst, ssem, rsem, device):
        copy = pltpu.make_async_remote_copy(
            src_ref=src, dst_ref=dst, send_sem=ssem, recv_sem=rsem,
            device_id=device, device_id_type=MESH,
        )
        copy.start()
        sent.append(copy)

    def arrived(dst, rsem):
        pltpu.make_async_remote_copy(
            src_ref=dst, dst_ref=dst, send_sem=s1.at[0, 0], recv_sem=rsem,
            device_id=sibling, device_id_type=MESH,
        ).wait_recv()

    order = list(range(1, n_dp)) + [0]
    hops = list(range(1, n_y)) + [0]

    def target(j):
        return lax.rem(dp + j, n_dp)

    def column(k):
        return lax.rem(y + k, n_y)

    for k in hops:
        for j in order:
            slot = target(j) * n_f + column(k) * CORES + 1 - core
            send(g_ref.at[slot], r1.at[j, k], s1.at[j, k], q1.at[j, k], sibling)
    for k in hops[:-1]:
        for j in order:
            arrived(r1.at[j, k], q1.at[j, k])
            slot = target(j) * n_f + column(k) * CORES + core
            a1[j, k - 1] = (g_ref[slot].astype(F32) + r1[j, k].astype(F32)).astype(BF16)
            send(a1.at[j, k - 1], r2.at[j, k - 1], s2.at[j, k - 1], q2.at[j, k - 1],
                 (dp, column(k) * CORES + core))
    for j in order:
        arrived(r1.at[j, 0], q1.at[j, 0])
        slot = target(j) * n_f + place
        total = g_ref[slot].astype(F32) + r1[j, 0].astype(F32)
        for k in hops[:-1]:
            arrived(r2.at[j, k - 1], q2.at[j, k - 1])
            total = total + r2[j, k - 1].astype(F32)
        if j:
            a2[j - 1] = total.astype(BF16)
            send(a2.at[j - 1], r3.at[j - 1], s3.at[j - 1], q3.at[j - 1], (target(j), place))
        else:
            o_ref[...] = total
    for j in order[:-1]:
        arrived(r3.at[j - 1], q3.at[j - 1])
        o_ref[...] += r3[j - 1].astype(F32)
    at = 0
    for out in outs:
        out[...] = o_ref[at : at + out.shape[0], :]
        at += tall(out.shape[0])
    for copy in sent:
        copy.wait_send()


def scatter_sum(terms, n_dp, n_f):
    n_y = n_f // CORES
    block = (sum(tall(t.shape[1]) for t in terms), LANES)
    far = max(n_y - 1, 1)
    dma = pltpu.SemaphoreType.DMA
    return pl.pallas_call(
        lambda *refs: scatter_kernel(n_dp, n_y, len(terms), *refs),
        out_shape=[jax.ShapeDtypeStruct(t.shape[1:], F32) for t in terms],
        in_specs=[pl.BlockSpec(memory_space=pltpu.VMEM)] * len(terms),
        out_specs=[pl.BlockSpec(memory_space=pltpu.VMEM)] * len(terms),
        scratch_shapes=[
            pltpu.VMEM((n_dp * n_f, *block), BF16),
            pltpu.VMEM(block, F32),
            pltpu.VMEM((n_dp, n_y, *block), BF16),
            pltpu.VMEM((n_dp, far, *block), BF16),
            pltpu.VMEM((n_dp, far, *block), BF16),
            pltpu.VMEM((n_dp - 1, *block), BF16),
            pltpu.VMEM((n_dp - 1, *block), BF16),
            dma((n_dp, n_y)), dma((n_dp, far)), dma((n_dp - 1,)),
            dma((n_dp, n_y)), dma((n_dp, far)), dma((n_dp - 1,)),
        ],
        compiler_params=pltpu.CompilerParams(
            collective_id=1, has_side_effects=True, vmem_limit_bytes=40 * 1024 * 1024
        ),
    )(*terms)


def lanes_of(size):
    return (size + LANES - 1) // LANES


def to_rows(values, count):
    flat = values.reshape(count, -1)
    size = flat.shape[1]
    if size % LANES:
        flat = jnp.pad(flat, ((0, 0), (0, lanes_of(size) * LANES - size)))
    else:
        flat = values
    return flat.reshape(count, lanes_of(size), LANES)


def tall(height):
    return (height + 15) // 16 * 16


def unpack(rows, sizes):
    outs, at = [], 0
    for size in sizes:
        height = lanes_of(size)
        piece = rows[:, at : at + height]
        if size % LANES:
            piece = piece.reshape(rows.shape[0], height * LANES)[:, :size]
        outs.append(piece)
        at += tall(height)
    return outs


def body(n_dp, n_f, tokens, image_count, w_qkv, w_out, w_fc1, w_fc2, norm_bias, cotangent):
    slots, seq, width = tokens.shape
    shards = (w_qkv, w_out, w_fc1, w_fc2, norm_bias)
    sizes = [s.shape[0] for s in shards]
    devices = n_dp * n_f
    gathered = gather_all([to_rows(p, 1)[0] for p in shards], n_dp, n_f)
    parts = unpack(gathered, sizes)
    hidden = sizes[2] * devices // width
    wqkv = parts[0].reshape(width, 3 * width)
    wout = parts[1].reshape(width, width)
    wup = parts[2].reshape(width, hidden)
    wdown = parts[3].reshape(hidden, width)
    vec = parts[4].astype(F32).reshape(-1)
    small = jnp.concatenate([vec[: 7 * width], vec[7 * width + hidden :]]).reshape(8, width)
    bup = vec[7 * width : 7 * width + hidden].reshape(1, hidden)
    output, grad_tokens, gqkv, gout, gup, gdown, gsmall, gbup = run_layer(
        image_count, tokens, cotangent, wqkv, wout, wup, wdown, small, bup
    )
    flat = gsmall.reshape(-1)
    gvec = jnp.concatenate([flat[: 7 * width], gbup.reshape(-1), flat[7 * width :]]).astype(BF16)
    terms = [to_rows(g, devices) for g in (gqkv, gout, gup, gdown, gvec)]
    summed = scatter_sum(terms, n_dp, n_f)
    grads = [g.reshape(-1)[:size] for g, size in zip(summed, sizes)]
    return (output, grad_tokens, *grads)


def solution(mesh):
    both = P(("dp", "fsdp"))
    images = P(("dp", "fsdp"), None, None)
    sizes = (mesh.shape["dp"], mesh.shape["fsdp"])
    return jax.shard_map(
        functools.partial(body, *sizes),
        mesh=mesh,
        in_specs=(images, both, both, both, both, both, both, images),
        out_specs=(images, images, both, both, both, both, both),
        check_vma=False,
    )
```

```python
import functools
import math

import jax
import jax.numpy as jnp
from jax import lax
from jax.experimental import pallas as pl
from jax.experimental.pallas import tpu as pltpu
from jax.sharding import PartitionSpec as P

HEADS = 6
HEAD_DIM = 64
EPS = 1e-06
F32 = jnp.float32
BF16 = jnp.bfloat16


def mm(a, b):
    return lax.dot_general(a, b, (((1,), (0,)), ((), ())), preferred_element_type=F32)


def mm_t(a, b):
    return lax.dot_general(a, b, (((1,), (1,)), ((), ())), preferred_element_type=F32)


def t_mm(a, b):
    return lax.dot_general(a, b, (((0,), (0,)), ((), ())), preferred_element_type=F32)


def norm_parts(values, width):
    mean = jnp.sum(values, axis=-1, keepdims=True) * (1.0 / width)
    center = values - mean
    var = jnp.sum(center * center, axis=-1, keepdims=True) * (1.0 / width)
    inverse = lax.rsqrt(var + EPS)
    return center * inverse, inverse


def norm_back(upstream, normed, inverse, gain, width):
    scaled = upstream * gain
    m1 = jnp.sum(scaled, axis=-1, keepdims=True) * (1.0 / width)
    m2 = jnp.sum(scaled * normed, axis=-1, keepdims=True) * (1.0 / width)
    return inverse * (scaled - m1 - normed * m2)


def gelu_both(z):
    ez = jnp.exp2(z * z * (-0.5 * 1.4426950408889634))
    d = 1.0 + (0.3275911 * 0.7071067811865476) * jnp.abs(z)
    t = pl.reciprocal(d, approx=True)
    t = t * (2.0 - d * t)
    poly = (((0.5307027145 * t - 0.7265760135) * t + 0.7107068705) * t - 0.142248368) * t + 0.127414796
    half = poly * t * ez
    cumul = jnp.where(z >= 0.0, 1.0 - half, half)
    return z * cumul, cumul + z * (ez * 0.3989422804014327)


def layer_kernel(
    count_ref, x_ref, ct_ref, wqkv_ref, wout_ref, wup_ref, wdown_ref, small_ref, bup_ref,
    out_ref, gx_ref, oqkv_ref, oout_ref, oup_ref, odown_ref, gsmall_ref, gbup_ref,
    gqkv_ref, gout_ref, gup_ref, gdown_ref,
    xs, cs, n1s, qs, ks, vs, pbs, os_, y1s, n2s, a1s, a2s, acts, dzs, dos, dqkvs,
):
    step = pl.program_id(0)
    seq, width = x_ref.shape[1], x_ref.shape[2]
    rows = xs.shape[0]
    hidden = wup_ref.shape[1]
    scale = 1.0 / math.sqrt(HEAD_DIM)

    @pl.when(step == 0)
    def _():
        xs[...] = jnp.zeros_like(xs)
        cs[...] = jnp.zeros_like(cs)
        for ref in (gqkv_ref, gout_ref, gup_ref, gdown_ref, gsmall_ref, gbup_ref):
            ref[...] = jnp.zeros_like(ref)

    live = step < count_ref[0]

    @pl.when(jnp.logical_not(live))
    def _():
        out_ref[...] = jnp.zeros_like(out_ref)
        gx_ref[...] = jnp.zeros_like(gx_ref)

    @pl.when(live)
    def _():
        xs[0:seq, :] = x_ref[0]
        cs[0:seq, :] = ct_ref[0]
        g1, c1 = small_ref[0:1, :], small_ref[1:2, :]
        bq, bv, bo = small_ref[2:3, :], small_ref[3:4, :], small_ref[4:5, :]
        g2, c2, b2 = small_ref[5:6, :], small_ref[6:7, :], small_ref[7:8, :]
        n1, inv1 = norm_parts(xs[...].astype(F32), width)
        n1s[...] = n1
        a1s[...] = (n1 * g1 + c1).astype(BF16)
        qs[...] = ((mm(a1s[...], wqkv_ref[:, :width]) + bq).astype(BF16).astype(F32) * scale).astype(BF16)
        ks[...] = mm(a1s[...], wqkv_ref[:, width : 2 * width]).astype(BF16)
        vs[...] = (mm(a1s[...], wqkv_ref[:, 2 * width :]) + bv).astype(BF16)
        lane = lax.broadcasted_iota(jnp.int32, (rows, 2 * HEAD_DIM), 1)
        halves = (lane < HEAD_DIM, lane >= HEAD_DIM)
        whole_rows = seq // 8 * 8
        keyrow = whole_rows + lax.broadcasted_iota(jnp.int32, (rows - whole_rows, rows), 0)
        zero = jnp.zeros((rows, 2 * HEAD_DIM), BF16)
        for pair in range(HEADS // 2):
            cols = slice(pair * 2 * HEAD_DIM, (pair + 1) * 2 * HEAD_DIM)
            qp, kp, vp = qs[:, cols], ks[:, cols], vs[:, cols]
            both = None
            twice = mm_t(jnp.concatenate([jnp.where(m, kp, zero) for m in halves], axis=0), qp)
            for h in range(2):
                vm = jnp.where(halves[h], vp, zero)
                scores = twice[h * rows : (h + 1) * rows]
                scores = jnp.concatenate(
                    [scores[:whole_rows], jnp.where(keyrow < seq, scores[whole_rows:], -1e30)], axis=0
                )
                top = jnp.max(scores, axis=0, keepdims=True)
                expo = jnp.exp(scores - top)
                total = jnp.sum(expo, axis=0, keepdims=True)
                prob = expo * (1.0 / total)
                pbs[pair * 2 + h] = prob.astype(BF16)
                part = t_mm(pbs[pair * 2 + h], vm)
                both = part if both is None else both + part
            os_[:, cols] = both.astype(BF16)
        y1 = xs[...].astype(F32) + (mm(os_[...], wout_ref[...]) + bo)
        y1s[...] = y1
        n2, inv2 = norm_parts(y1, width)
        n2s[...] = n2
        a2s[...] = (n2 * g2 + c2).astype(BF16)
        tile = 256
        for j in range(hidden // tile):
            cols = slice(j * tile, (j + 1) * tile)
            z = mm(a2s[...], wup_ref[:, cols]) + bup_ref[:, cols]
            act, slope = gelu_both(z)
            acts[:, cols] = act.astype(BF16)
            dz = (mm_t(cs[...], wdown_ref[cols, :]) * slope).astype(BF16)
            dzs[:, cols] = dz
            gbup_ref[:, cols] += jnp.sum(dz.astype(F32), axis=0, keepdims=True)
        y = y1s[...] + mm(acts[...], wdown_ref[...]) + b2
        out_ref[0] = y[:seq].astype(BF16)
        gdown_ref[...] += t_mm(cs[...], acts[...])
        gup_ref[...] += t_mm(a2s[...], dzs[...])
        da2 = mm_t(dzs[...], wup_ref[...])
        ct = cs[...].astype(F32)
        n2 = n2s[...]
        gsmall_ref[7:8, :] += jnp.sum(ct, axis=0, keepdims=True)
        gsmall_ref[5:6, :] += jnp.sum(da2 * n2, axis=0, keepdims=True)
        gsmall_ref[6:7, :] += jnp.sum(da2, axis=0, keepdims=True)
        dy1 = ct + norm_back(da2, n2, inv2, g2, width)
        y1s[...] = dy1
        da = dy1.astype(BF16)
        gsmall_ref[4:5, :] += jnp.sum(da.astype(F32), axis=0, keepdims=True)
        gout_ref[...] += t_mm(os_[...], da)
        dos[...] = mm_t(da, wout_ref[...]).astype(BF16)
        for pair in range(HEADS // 2):
            cols = slice(pair * 2 * HEAD_DIM, (pair + 1) * 2 * HEAD_DIM)
            qp, kp, vp, dop = qs[:, cols], ks[:, cols], vs[:, cols], dos[:, cols]
            dq = dk = dv = None
            twice = mm_t(jnp.concatenate([jnp.where(m, vp, zero) for m in halves], axis=0), dop)
            for h in range(2):
                qm = jnp.where(halves[h], qp, zero)
                km = jnp.where(halves[h], kp, zero)
                dom = jnp.where(halves[h], dop, zero)
                pb = pbs[pair * 2 + h]
                prob = pb.astype(F32)
                dp = twice[h * rows : (h + 1) * rows]
                inner = jnp.sum(prob * dp, axis=0, keepdims=True)
                ds = (prob * (dp - inner)).astype(BF16)
                dv_h = mm(pb, dom)
                dk_h = mm(ds, qm)
                dq_h = t_mm(ds, km)
                dq = dq_h if dq is None else dq + dq_h
                dk = dk_h if dk is None else dk + dk_h
                dv = dv_h if dv is None else dv + dv_h
            base = pair * 2 * HEAD_DIM
            dqkvs[:, base : base + 2 * HEAD_DIM] = (dq * scale).astype(BF16)
            dqkvs[:, width + base : width + base + 2 * HEAD_DIM] = dk.astype(BF16)
            dqkvs[:, 2 * width + base : 2 * width + base + 2 * HEAD_DIM] = dv.astype(BF16)
        gsmall_ref[2:3, :] += jnp.sum(dqkvs[:, :width].astype(F32), axis=0, keepdims=True)
        gsmall_ref[3:4, :] += jnp.sum(dqkvs[:, 2 * width :].astype(F32), axis=0, keepdims=True)
        gqkv_ref[...] += t_mm(a1s[...], dqkvs[...])
        da1 = mm_t(dqkvs[...], wqkv_ref[...])
        n1 = n1s[...]
        gsmall_ref[0:1, :] += jnp.sum(da1 * n1, axis=0, keepdims=True)
        gsmall_ref[1:2, :] += jnp.sum(da1, axis=0, keepdims=True)
        gx = y1s[...] + norm_back(da1, n1, inv1, g1, width)
        gx_ref[0] = gx[:seq].astype(BF16)

    @pl.when(step == pl.num_programs(0) - 1)
    def _():
        oqkv_ref[...] = gqkv_ref[...].astype(BF16)
        oout_ref[...] = gout_ref[...].astype(BF16)
        oup_ref[...] = gup_ref[...].astype(BF16)
        for j in range(hidden // width):
            block = slice(j * width, (j + 1) * width)
            odown_ref[block, :] = gdown_ref[:, block].T.astype(BF16)


def run_layer(count, tokens, cotangent, wqkv, wout, wup, wdown, small, bup):
    slots, seq, width = tokens.shape
    hidden = wup.shape[1]
    rows = (seq + 15) // 16 * 16

    def whole(shape):
        return pl.BlockSpec(shape, lambda i, c: (0,) * len(shape), pipeline_mode=pl.Buffered(1))

    def image():
        return pl.BlockSpec((1, seq, width), lambda i, c: (i, 0, 0))

    return pl.pallas_call(
        layer_kernel,
        grid_spec=pltpu.PrefetchScalarGridSpec(
            num_scalar_prefetch=1,
            grid=(slots,),
            in_specs=[
                image(), image(),
                whole((width, 3 * width)), whole((width, width)), whole((width, hidden)),
                whole((hidden, width)), whole((8, width)), whole((1, hidden)),
            ],
            out_specs=[
                image(), image(),
                whole((width, 3 * width)), whole((width, width)), whole((width, hidden)),
                whole((hidden, width)), whole((8, width)), whole((1, hidden)),
            ],
            scratch_shapes=[
                pltpu.VMEM((width, 3 * width), F32),
                pltpu.VMEM((width, width), F32),
                pltpu.VMEM((width, hidden), F32),
                pltpu.VMEM((width, hidden), F32),
                pltpu.VMEM((rows, width), BF16),
                pltpu.VMEM((rows, width), BF16),
                pltpu.VMEM((rows, width), F32),
                pltpu.VMEM((rows, width), BF16),
                pltpu.VMEM((rows, width), BF16),
                pltpu.VMEM((rows, width), BF16),
                pltpu.VMEM((HEADS, rows, rows), BF16),
                pltpu.VMEM((rows, width), BF16),
                pltpu.VMEM((rows, width), F32),
                pltpu.VMEM((rows, width), F32),
                pltpu.VMEM((rows, width), BF16),
                pltpu.VMEM((rows, width), BF16),
                pltpu.VMEM((rows, hidden), BF16),
                pltpu.VMEM((rows, hidden), BF16),
                pltpu.VMEM((rows, width), BF16),
                pltpu.VMEM((rows, 3 * width), BF16),
            ],
        ),
        out_shape=[
            jax.ShapeDtypeStruct(tokens.shape, BF16),
            jax.ShapeDtypeStruct(tokens.shape, BF16),
            jax.ShapeDtypeStruct((width, 3 * width), BF16),
            jax.ShapeDtypeStruct((width, width), BF16),
            jax.ShapeDtypeStruct((width, hidden), BF16),
            jax.ShapeDtypeStruct((hidden, width), BF16),
            jax.ShapeDtypeStruct((8, width), F32),
            jax.ShapeDtypeStruct((1, hidden), F32),
        ],
        compiler_params=pltpu.CompilerParams(
            dimension_semantics=("arbitrary",), vmem_limit_bytes=48 * 1024 * 1024
        ),
    )(count, tokens, cotangent, wqkv, wout, wup, wdown, small, bup)


MESH = pl.DeviceIdType.MESH
CORES = 2
LANES = 128


def greet(n_dp, n_y, dp, y, core):
    barrier = pltpu.get_barrier_semaphore()
    pl.semaphore_signal(
        barrier, inc=1, device_id=(dp, y * CORES + 1 - core), device_id_type=MESH
    )
    for k in range(1, n_y):
        other = lax.rem(y + k, n_y)
        pl.semaphore_signal(barrier, inc=1, device_id=(dp, other * CORES + core), device_id_type=MESH)
    for k in range(1, n_dp):
        other = lax.rem(dp + k, n_dp)
        pl.semaphore_signal(barrier, inc=1, device_id=(other, y * CORES + core), device_id_type=MESH)
    pl.semaphore_wait(barrier, n_dp + n_y - 1)


def gather_kernel(n_dp, n_y, count, *refs):
    parts, (o_ref, x_ref, own_sem, dp_send, y_send, core_send, recv_sem) = refs[:count], refs[count:]
    fill(x_ref, parts)
    dp = lax.axis_index("dp")
    place = lax.axis_index("fsdp")
    y, core = place // CORES, lax.rem(place, CORES)
    n_f = n_y * CORES
    greet(n_dp, n_y, dp, y, core)
    me = dp * n_f + place
    sent = []

    def send(src, slot, sem, device):
        copy = pltpu.make_async_remote_copy(
            src_ref=src, dst_ref=o_ref.at[slot], send_sem=sem, recv_sem=recv_sem.at[slot],
            device_id=device, device_id_type=MESH,
        )
        copy.start()
        sent.append(copy)

    def arrived(slot):
        pltpu.make_async_remote_copy(
            src_ref=x_ref, dst_ref=o_ref.at[slot], send_sem=own_sem, recv_sem=recv_sem.at[slot],
            device_id=(dp, y * CORES + 1 - core), device_id_type=MESH,
        ).wait_recv()

    own = pltpu.make_async_copy(x_ref, o_ref.at[me], own_sem)
    own.start()
    for k in range(1, n_dp):
        send(x_ref, me, dp_send.at[k], (lax.rem(dp + k, n_dp), place))
    for j in range(n_dp):
        slot = lax.rem(dp + n_dp - j, n_dp) * n_f + place
        if j:
            arrived(slot)
        src = o_ref.at[slot] if j else x_ref
        for k in range(1, n_y):
            send(src, slot, y_send.at[j, k], (dp, lax.rem(y + k, n_y) * CORES + core))
        send(src, slot, core_send.at[j, 0], (dp, y * CORES + 1 - core))
    for j in range(n_dp):
        for k in range(1, n_y):
            slot = lax.rem(dp + n_dp - j, n_dp) * n_f + lax.rem(y + n_y - k, n_y) * CORES + core
            arrived(slot)
            send(o_ref.at[slot], slot, core_send.at[j, k], (dp, y * CORES + 1 - core))
    for j in range(n_dp):
        for k in range(n_y):
            slot = lax.rem(dp + n_dp - j, n_dp) * n_f + lax.rem(y + n_y - k, n_y) * CORES + 1 - core
            arrived(slot)
    own.wait()
    for copy in sent:
        copy.wait_send()


def fill(block, parts):
    at = 0
    for part in parts:
        block[at : at + part.shape[0], :] = part[...]
        at += tall(part.shape[0])


def gather_all(parts, n_dp, n_f):
    n_y = n_f // CORES
    height = sum(tall(p.shape[0]) for p in parts)
    block = (height, LANES)
    return pl.pallas_call(
        lambda *refs: gather_kernel(n_dp, n_y, len(parts), *refs),
        out_shape=jax.ShapeDtypeStruct((n_dp * n_f, *block), BF16),
        in_specs=[pl.BlockSpec(memory_space=pltpu.VMEM)] * len(parts),
        out_specs=pl.BlockSpec(memory_space=pl.ANY),
        scratch_shapes=[
            pltpu.VMEM(block, BF16),
            pltpu.SemaphoreType.DMA,
            pltpu.SemaphoreType.DMA((n_dp,)),
            pltpu.SemaphoreType.DMA((n_dp, n_y)),
            pltpu.SemaphoreType.DMA((n_dp, n_y)),
            pltpu.SemaphoreType.DMA((n_dp * n_f,)),
        ],
        compiler_params=pltpu.CompilerParams(collective_id=0, has_side_effects=True),
    )(*parts)


def scatter_kernel(n_dp, n_y, count, *refs):
    parts, outs = refs[:count], refs[count : 2 * count]
    g_ref, o_ref, r1, a1, r2, a2, r3, s1, s2, s3, q1, q2, q3 = refs[2 * count :]

    def fill_slot(slot, carry):
        at = 0
        for part in parts:
            g_ref[slot, at : at + part.shape[1], :] = part[slot]
            at += tall(part.shape[1])
        return carry

    lax.fori_loop(0, n_dp * n_y * CORES, fill_slot, 0)
    dp = lax.axis_index("dp")
    place = lax.axis_index("fsdp")
    y, core = place // CORES, lax.rem(place, CORES)
    n_f = n_y * CORES
    greet(n_dp, n_y, dp, y, core)
    sibling = (dp, y * CORES + 1 - core)
    sent = []

    def send(src, dst, ssem, rsem, device):
        copy = pltpu.make_async_remote_copy(
            src_ref=src, dst_ref=dst, send_sem=ssem, recv_sem=rsem,
            device_id=device, device_id_type=MESH,
        )
        copy.start()
        sent.append(copy)

    def arrived(dst, rsem):
        pltpu.make_async_remote_copy(
            src_ref=dst, dst_ref=dst, send_sem=s1.at[0, 0], recv_sem=rsem,
            device_id=sibling, device_id_type=MESH,
        ).wait_recv()

    order = list(range(1, n_dp)) + [0]
    hops = list(range(1, n_y)) + [0]

    def target(j):
        return lax.rem(dp + j, n_dp)

    def column(k):
        return lax.rem(y + k, n_y)

    for k in hops:
        for j in order:
            slot = target(j) * n_f + column(k) * CORES + 1 - core
            send(g_ref.at[slot], r1.at[j, k], s1.at[j, k], q1.at[j, k], sibling)
    for k in hops[:-1]:
        for j in order:
            arrived(r1.at[j, k], q1.at[j, k])
            slot = target(j) * n_f + column(k) * CORES + core
            a1[j, k - 1] = (g_ref[slot].astype(F32) + r1[j, k].astype(F32)).astype(BF16)
            send(a1.at[j, k - 1], r2.at[j, k - 1], s2.at[j, k - 1], q2.at[j, k - 1],
                 (dp, column(k) * CORES + core))
    for j in order:
        arrived(r1.at[j, 0], q1.at[j, 0])
        slot = target(j) * n_f + place
        total = g_ref[slot].astype(F32) + r1[j, 0].astype(F32)
        for k in hops[:-1]:
            arrived(r2.at[j, k - 1], q2.at[j, k - 1])
            total = total + r2[j, k - 1].astype(F32)
        if j:
            a2[j - 1] = total.astype(BF16)
            send(a2.at[j - 1], r3.at[j - 1], s3.at[j - 1], q3.at[j - 1], (target(j), place))
        else:
            o_ref[...] = total
    for j in order[:-1]:
        arrived(r3.at[j - 1], q3.at[j - 1])
        o_ref[...] += r3[j - 1].astype(F32)
    at = 0
    for out in outs:
        out[...] = o_ref[at : at + out.shape[0], :]
        at += tall(out.shape[0])
    for copy in sent:
        copy.wait_send()


def scatter_sum(terms, n_dp, n_f):
    n_y = n_f // CORES
    block = (sum(tall(t.shape[1]) for t in terms), LANES)
    far = max(n_y - 1, 1)
    dma = pltpu.SemaphoreType.DMA
    return pl.pallas_call(
        lambda *refs: scatter_kernel(n_dp, n_y, len(terms), *refs),
        out_shape=[jax.ShapeDtypeStruct(t.shape[1:], F32) for t in terms],
        in_specs=[pl.BlockSpec(memory_space=pltpu.VMEM)] * len(terms),
        out_specs=[pl.BlockSpec(memory_space=pltpu.VMEM)] * len(terms),
        scratch_shapes=[
            pltpu.VMEM((n_dp * n_f, *block), BF16),
            pltpu.VMEM(block, F32),
            pltpu.VMEM((n_dp, n_y, *block), BF16),
            pltpu.VMEM((n_dp, far, *block), BF16),
            pltpu.VMEM((n_dp, far, *block), BF16),
            pltpu.VMEM((n_dp - 1, *block), BF16),
            pltpu.VMEM((n_dp - 1, *block), BF16),
            dma((n_dp, n_y)), dma((n_dp, far)), dma((n_dp - 1,)),
            dma((n_dp, n_y)), dma((n_dp, far)), dma((n_dp - 1,)),
        ],
        compiler_params=pltpu.CompilerParams(
            collective_id=1, has_side_effects=True, vmem_limit_bytes=40 * 1024 * 1024
        ),
    )(*terms)


def lanes_of(size):
    return (size + LANES - 1) // LANES


def to_rows(values, count):
    flat = values.reshape(count, -1)
    size = flat.shape[1]
    if size % LANES:
        flat = jnp.pad(flat, ((0, 0), (0, lanes_of(size) * LANES - size)))
    else:
        flat = values
    return flat.reshape(count, lanes_of(size), LANES)


def tall(height):
    return (height + 15) // 16 * 16


def unpack(rows, sizes):
    outs, at = [], 0
    for size in sizes:
        height = lanes_of(size)
        piece = rows[:, at : at + height]
        if size % LANES:
            piece = piece.reshape(rows.shape[0], height * LANES)[:, :size]
        outs.append(piece)
        at += tall(height)
    return outs


def body(n_dp, n_f, tokens, image_count, w_qkv, w_out, w_fc1, w_fc2, norm_bias, cotangent):
    slots, seq, width = tokens.shape
    shards = (w_qkv, w_out, w_fc1, w_fc2, norm_bias)
    sizes = [s.shape[0] for s in shards]
    devices = n_dp * n_f
    gathered = gather_all([to_rows(p, 1)[0] for p in shards], n_dp, n_f)
    parts = unpack(gathered, sizes)
    hidden = sizes[2] * devices // width
    wqkv = parts[0].reshape(width, 3 * width)
    wout = parts[1].reshape(width, width)
    wup = parts[2].reshape(width, hidden)
    wdown = parts[3].reshape(hidden, width)
    vec = parts[4].astype(F32).reshape(-1)
    small = jnp.concatenate([vec[: 7 * width], vec[7 * width + hidden :]]).reshape(8, width)
    bup = vec[7 * width : 7 * width + hidden].reshape(1, hidden)
    output, grad_tokens, gqkv, gout, gup, gdown, gsmall, gbup = run_layer(
        image_count, tokens, cotangent, wqkv, wout, wup, wdown, small, bup
    )
    flat = gsmall.reshape(-1)
    gvec = jnp.concatenate([flat[: 7 * width], gbup.reshape(-1), flat[7 * width :]]).astype(BF16)
    terms = [to_rows(g, devices) for g in (gqkv, gout, gup, gdown, gvec)]
    summed = scatter_sum(terms, n_dp, n_f)
    grads = [g.reshape(-1)[:size] for g, size in zip(summed, sizes)]
    return (output, grad_tokens, *grads)


def solution(mesh):
    both = P(("dp", "fsdp"))
    images = P(("dp", "fsdp"), None, None)
    sizes = (mesh.shape["dp"], mesh.shape["fsdp"])
    return jax.shard_map(
        functools.partial(body, *sizes),
        mesh=mesh,
        in_specs=(images, both, both, both, both, both, both, images),
        out_specs=(images, images, both, both, both, both, both),
        check_vma=False,
    )
```
